32 devices in a mesh: ctx: 8 (over y, x, core), kv: 4 (over z).
Axes of the slice: x: 2, y: 2, z: 4, core: 2. Of those that a mesh axis runs over, the one named last changes fastest.
Arguments:
- tokens: bfloat16 [128, 16384], P('kv', 'ctx'), may hold values from -6 to 6
- qkv_weight: bfloat16 [16384, 9216], P('ctx', 'kv'), may hold values from -2 to 2
- cache_keys: bfloat16 [16384, 512], P('ctx', 'kv'), may hold values from -8 to 8
- cache_values: bfloat16 [16384, 512], P('ctx', 'kv'), may hold values from -6 to 6
- cache_fill: int32 [8], replicated, may hold values from 1 to 2016, as said below
- slot_owner: int32 [128], replicated, may hold values from 0 to 7, as said below
- new_positions: int32 [128], replicated, may hold values from 0 to 127, each once
Outputs:
- attended: bfloat16 [128, 8192], P('ctx', 'kv')
- keys_after: bfloat16 [16384, 512], P('ctx', 'kv')
- values_after: bfloat16 [16384, 512], P('ctx', 'kv')
The draws below stay inside these ranges and needn't reach their ends.
Inputs may be any that keep to these rules, and one draw needn't show every extreme that they name: Each device's first cache_fill slots hold entries that precede every new token in the sequence; one device's count equals 2016 in every draw. `slot_owner`: in each device's aligned block of 16 new tokens no owner appears more than 4 times; one owner, the same for all blocks, appears exactly 4 times in every block. `new_positions`: each offset appears once.
All inputs are finite; a program needn't handle non-finite values.
Results may differ from the reference program's by a relative error of at most 0.015.
The reference program's roundings to bfloat16 on the way count: a program that leaves them out, or rounds other values in their place, can miss the bound.
Values may be sent and summed in bfloat16 or wider, within the bound.
No kernel may reach another device: no remote copies, remote signals or barrier semaphores. Data moves between devices by JAX's collectives and lax.ppermute only.
A program may use at most 64 MiB of HBM per device.

```python
import math
import jax
import jax.numpy as jnp
from jax import lax

D = 16384
HQ = 16
HD = 128
KVH = 4
NEW_DEV = 16
NEW = 128
CAP = 4
CACHE_DEV = 2048
SLOTS = 16384
MAXF = 2016


def draw_qkv_weight(key, part):
    lane_width = (HQ + 2) * HD
    columns = KVH * lane_width
    column = jnp.arange(columns)
    within_lane = column % lane_width
    is_query = within_lane < HQ * HD
    base_scale = jnp.where(is_query, 3.0, 1.0) / math.sqrt(D)
    key_values = jax.random.fold_in(key, 0)
    values = jnp.clip(jax.random.normal(key_values, (D, columns), jnp.float32), -6.0, 6.0)
    column_scale = base_scale
    return (values * column_scale[None, :]).astype(jnp.bfloat16)


def draw_cache_keys(key, part):
    row_width = KVH * HD
    first_key = jax.random.fold_in(key, 0)
    return jnp.clip(jax.random.normal(first_key, (SLOTS, row_width), jnp.float32), -6.0, 6.0).astype(jnp.bfloat16)


def draw_cache_fill(key, part):
    peer_count = NEW // NEW_DEV
    spread_key, top_key = jax.random.split(key)
    spread_draw = jax.random.randint(spread_key, (peer_count,), 0, 256)
    filled = 1 + spread_draw * spread_draw * (MAXF - 1) // 65536
    fullest = jax.random.randint(top_key, (), 0, peer_count)
    return jnp.where(jnp.arange(peer_count) == fullest, MAXF, filled).astype(jnp.int32)


def draw_slot_owner(key, part):
    peer_count = NEW // NEW_DEV
    hot_key, rest_key = jax.random.split(key)
    busiest = jax.random.randint(hot_key, (), 0, peer_count)

    def one_block(block_key):
        order_key, slot_key = jax.random.split(block_key)
        others = jax.random.permutation(slot_key, (peer_count - 1) * CAP)[:NEW_DEV - CAP] // CAP
        others = others + (others >= busiest).astype(jnp.int32)
        assigned = jnp.concatenate([jnp.full((CAP,), busiest, jnp.int32), others.astype(jnp.int32)])
        shuffle = jax.random.permutation(order_key, NEW_DEV)
        return assigned[shuffle]
    return jax.vmap(one_block)(jax.random.split(rest_key, peer_count)).reshape(NEW).astype(jnp.int32)


def steps_of(key, dims, cuts, low, largest):
    level, own = 1.0, jax.random.fold_in(key, 6)
    for axis_at, shards_of in cuts:
        draws = jnp.exp(jax.random.uniform(jax.random.fold_in(own, axis_at), (shards_of,), jnp.float32, low / len(cuts), largest / len(cuts)))
        level = level * jnp.repeat(draws, dims[axis_at] // shards_of).reshape([-1 if axis == axis_at else 1 for axis in range(len(dims))])
    return level


def scatter_about(own_key, extent, deviation, limit, cuts=(), held_as=jnp.bfloat16):
    loudness = steps_of(own_key, extent, cuts, -0.22, 0.18) if cuts else 1.0
    entries = jax.random.normal(own_key, extent, jnp.float32) * deviation * loudness
    return jnp.minimum(jnp.maximum(entries, -limit), limit).astype(held_as)


def setup_inputs(seed: int = 0) -> dict:
    splits = jax.random.split(jax.random.key(seed), 8)
    tokens = scatter_about(splits[0], (NEW, D), 1.0, 6.0, ((0, 4), (1, 8)))
    qkv_weight = draw_qkv_weight(jax.random.fold_in(splits[7], 71), 0)
    cache_keys = draw_cache_keys(jax.random.fold_in(splits[7], 71), 0)
    cache_values = scatter_about(splits[3], (SLOTS, KVH * HD), 1.0, 6.0, ((0, 8), (1, 4)))
    cache_fill = draw_cache_fill(jax.random.fold_in(splits[7], 71), 0)
    slot_owner = draw_slot_owner(jax.random.fold_in(splits[7], 71), 0)
    new_positions = jax.random.permutation(splits[6], NEW).astype(jnp.int32)
    return {"tokens": tokens, "qkv_weight": qkv_weight, "cache_keys": cache_keys, "cache_values": cache_values, "cache_fill": cache_fill, "slot_owner": slot_owner, "new_positions": new_positions}


rope_base = 500000.0
far_away = 1 << 30

def rotate(vectors, offsets):
    head_dim = vectors.shape[-1]
    half_dim = head_dim // 2
    freqs = jnp.exp(jnp.arange(half_dim, dtype=jnp.float32) * (-2.0 * math.log(rope_base) / head_dim))
    angles = offsets.astype(jnp.float32)[:, None] * freqs[None, :]
    cosines = jnp.cos(angles)[:, None, :]
    sine_part = jnp.sin(angles)[:, None, :]
    front_half = vectors[..., :half_dim]
    back_half = vectors[..., half_dim:]
    return jnp.concatenate([front_half * cosines - back_half * sine_part, back_half * cosines + front_half * sine_part], -1)

def reference(tokens, qkv_weight, cache_keys, cache_values, cache_fill, slot_owner, new_positions):
    lane_width = (HQ + 2) * HD
    projected = jnp.dot(tokens, qkv_weight, preferred_element_type=jnp.float32).reshape(NEW, KVH, lane_width)
    absolute = (jnp.sum(cache_fill) + new_positions).astype(jnp.int32)
    queries = rotate(projected[:, :, :HQ * HD].reshape(NEW, KVH * HQ, HD), absolute).astype(jnp.bfloat16)
    keys_new = rotate(projected[:, :, HQ * HD:(HQ + 1) * HD], absolute).astype(jnp.bfloat16)
    values_new = projected[:, :, (HQ + 1) * HD:].astype(jnp.bfloat16)
    peer_count = NEW // NEW_DEV
    one_hot = (slot_owner[:, None] == jnp.arange(peer_count, dtype=jnp.int32)[None, :]).astype(jnp.int32)
    earlier = jnp.cumsum(one_hot, 0) - one_hot
    rank_in = lax.optimization_barrier(jnp.sum(earlier * one_hot, 1))
    owner_fill = lax.optimization_barrier(jnp.sum(one_hot * cache_fill[None, :], 1))
    target = (slot_owner * CACHE_DEV + owner_fill + rank_in).astype(jnp.int32)
    keys_after = cache_keys.at[target].set(keys_new.reshape(NEW, KVH * HD))
    values_after = cache_values.at[target].set(values_new.reshape(NEW, KVH * HD))
    slot_iota = jnp.arange(SLOTS, dtype=jnp.int32)
    device_fill = jnp.repeat(cache_fill, CACHE_DEV)
    key_position = jnp.where(slot_iota % CACHE_DEV < device_fill, -1, far_away).astype(jnp.int32)
    key_position = key_position.at[target].set(absolute)
    lane_queries = queries.reshape(NEW, KVH, HQ, HD).transpose(1, 0, 2, 3)
    lane_keys = keys_after.reshape(SLOTS, KVH, HD).transpose(1, 0, 2)
    lane_values = values_after.reshape(SLOTS, KVH, HD).transpose(1, 0, 2)
    block_tokens = min(64, NEW)
    score_scale = 1.0 / math.sqrt(HD)

    def one_lane(operands):
        query_lane, key_lane, value_lane = operands

        def one_block(pieces):
            query_block, block_pos = pieces
            query_rows = query_block.reshape(block_tokens * HQ, HD)
            scores = jnp.dot(query_rows, key_lane.T, preferred_element_type=jnp.float32) * score_scale
            row_pos = jnp.repeat(block_pos, HQ)
            scores = jnp.where(key_position[None, :] <= row_pos[:, None], scores, -jnp.inf)
            row_max = lax.optimization_barrier(jnp.max(scores, 1, keepdims=True))
            weights = jnp.exp(scores - row_max)
            denominator = lax.optimization_barrier(jnp.sum(weights, 1, keepdims=True))
            mixed_out = jnp.dot(weights.astype(jnp.bfloat16), value_lane, preferred_element_type=jnp.float32) / denominator
            return mixed_out.astype(jnp.bfloat16).reshape(block_tokens, HQ * HD)
        blocks = query_lane.reshape(NEW // block_tokens, block_tokens, HQ, HD)
        block_positions = absolute.reshape(NEW // block_tokens, block_tokens)
        return lax.map(one_block, (blocks, block_positions)).reshape(NEW, HQ * HD)
    per_lane = lax.map(one_lane, (lane_queries, lane_keys, lane_values))
    attended = per_lane.transpose(1, 0, 2).reshape(NEW, KVH * HQ * HD)
    return (attended, keys_after, values_after)
```

```python
import functools
import math

import jax
import jax.numpy as jnp
from jax import lax
from jax.experimental import pallas as pl
from jax.experimental.pallas import tpu as pltpu
from jax.sharding import PartitionSpec as P

rope_base = 500000.0
lowest = -1e30
f32, bf16 = jnp.float32, jnp.bfloat16
in_vmem = pl.BlockSpec(memory_space=pltpu.VMEM)
in_smem = pl.BlockSpec(memory_space=pltpu.SMEM)


def project_kernel(place, *refs, peers, rows, half_blocks, width):
    parts, weight, keep, send, gathered = refs[:peers], *refs[peers:]
    step = pl.program_id(0)
    core, lane = place[0], place[1]

    @pl.when(step == 0)
    def _():
        for hop in range(peers):
            start = pl.multiple_of((lane ^ hop) * rows, rows)
            gathered[pl.ds(start, rows), :] = parts[hop][...]

    product = jnp.dot(gathered[...], weight[...], preferred_element_type=f32)

    @pl.when(step < half_blocks)
    def _():
        send[:, pl.ds(pl.multiple_of(step * width, width), width)] = product

    @pl.when(step == half_blocks)
    def _():
        send[:, half_blocks * width :] = product
        keep[:, half_blocks * width :] = product

    @pl.when(step > half_blocks)
    def _():
        start = (step - half_blocks - 1) * width
        keep[:, pl.ds(pl.multiple_of(start, width), width)] = product


def project(place, parts, weight, width):
    peers, (rows, depth) = len(parts), parts[0].shape
    columns = weight.shape[1]
    half_blocks = (columns // width - 1) // 2

    def weight_block(step, place):
        core = place[0]
        sent = (1 - core) * half_blocks + step
        kept = core * half_blocks + step - half_blocks - 1
        shared = 2 * half_blocks
        block = jnp.where(step < half_blocks, sent, jnp.where(step == half_blocks, shared, kept))
        return (0, block)

    whole = lambda step, place: (0, 0)
    out = jax.ShapeDtypeStruct((peers * rows, (half_blocks + 1) * width), f32)
    return pl.pallas_call(
        functools.partial(
            project_kernel, peers=peers, rows=rows, half_blocks=half_blocks, width=width
        ),
        out_shape=(out, out),
        grid_spec=pltpu.PrefetchScalarGridSpec(
            num_scalar_prefetch=1,
            grid=(2 * half_blocks + 1,),
            in_specs=[pl.BlockSpec((rows, depth), whole)] * peers
            + [pl.BlockSpec((depth, width), weight_block)],
            out_specs=(pl.BlockSpec(out.shape, whole), pl.BlockSpec(out.shape, whole)),
            scratch_shapes=[pltpu.VMEM((peers * rows, depth), bf16)],
        ),
        compiler_params=pltpu.CompilerParams(vmem_limit_bytes=24 << 20),
    )(place, *parts, weight)


def attend_kernel(place, fill, *refs, chips, heads, group, block, scale):
    projected, cosines, sines, allowed, keys_0, keys_1, values_0, values_1 = refs[:8]
    outs = refs[8 : 8 + chips]
    keys_new, values_new, query, peak, total, mixed, packed = refs[8 + chips :]
    tokens, head_dim = cosines.shape
    factor = scale * math.log2(math.e)

    def rotated(column):
        u = projected[:, column * head_dim : (column + 1) * head_dim]
        return (u * cosines[...] + pltpu.roll(u, head_dim // 2, 1) * sines[...]).astype(bf16)

    for head in range(heads):
        query[head * tokens : (head + 1) * tokens, :] = rotated(head)
    keys_new[...] = rotated(heads)
    values_new[...] = projected[:, (heads + 1) * head_dim :].astype(bf16)

    def scores_of(head, key_part):
        rows = query[head * tokens : (head + 1) * tokens, :]
        return lax.dot_general(
            rows, key_part, (((1,), (1,)), ((), ())), preferred_element_type=f32
        )

    def folded(weights):
        return functools.reduce(
            jnp.add,
            [
                weights[:, i * head_dim : (i + 1) * head_dim]
                for i in range(weights.shape[1] // head_dim)
            ],
        )

    attended_new = allowed[...] > 0.0
    for head in range(heads):
        at = slice(head * tokens, (head + 1) * tokens)
        scores = jnp.where(attended_new, scores_of(head, keys_new[...]), lowest)
        top = jnp.broadcast_to(jnp.max(scores, 1, keepdims=True), (tokens, head_dim))
        weights = jnp.where(attended_new, jnp.exp2((scores - top[:, :1]) * factor), 0.0)
        peak[at, :] = top
        total[at, :] = folded(weights)
        mixed[at, :] = jnp.dot(
            weights.astype(bf16), values_new[...], preferred_element_type=f32
        )

    def advance(keys, values, start, filled):
        key_part = keys[pl.ds(start, block), :]
        value_part = values[pl.ds(start, block), :]
        if filled is not None:
            slot = start + lax.broadcasted_iota(jnp.int32, (1, block), 1)
        for head in range(heads):
            at = slice(head * tokens, (head + 1) * tokens)
            scores = scores_of(head, key_part)
            if filled is not None:
                scores = jnp.where(slot < filled, scores, lowest)
            before = peak[at, :]
            top = jnp.maximum(before, jnp.max(scores, 1, keepdims=True))
            rescale = jnp.exp2((before - top) * factor)
            weights = jnp.exp2((scores - top[:, :1]) * factor)
            peak[at, :] = top
            total[at, :] = total[at, :] * rescale + folded(weights)
            mixed[at, :] = mixed[at, :] * rescale + jnp.dot(
                weights.astype(bf16), value_part, preferred_element_type=f32
            )

    for which, (keys, values) in enumerate(((keys_0, values_0), (keys_1, values_1))):
        filled = fill[which]
        full = filled // block

        @pl.loop(0, full)
        def _(step, keys=keys, values=values):
            advance(keys, values, pl.multiple_of(step * block, block), None)

        @pl.when(full * block < filled)
        def _(keys=keys, values=values, full=full, filled=filled):
            advance(keys, values, pl.multiple_of(full * block, block), filled)

    lane = lax.broadcasted_iota(jnp.int32, (tokens, head_dim), 1)
    logs = jnp.zeros((tokens, head_dim), f32)
    for head in range(heads):
        at = slice(head * tokens, (head + 1) * tokens)
        denominator = jnp.sum(total[at, :], 1, keepdims=True)
        packed[:, head * head_dim : (head + 1) * head_dim] = (mixed[at, :] / denominator).astype(
            bf16
        )
        level = peak[at, :] * factor + jnp.log2(denominator)
        logs = jnp.where(lane % heads == head, level, logs)
    first = logs.astype(bf16).astype(f32)
    second = (logs - first).astype(bf16).astype(f32)
    third = logs - first - second
    packed[:, heads * head_dim :] = jnp.where(
        lane < heads, first, jnp.where(lane < 2 * heads, second, third)
    ).astype(bf16)
    for hop in range(chips):
        start = pl.multiple_of((place[2] ^ hop) * group, group)
        outs[hop][...] = packed[pl.ds(start, group), :]


def attend(place, fill, projected, cosines, sines, allowed, caches, chips, group):
    tokens, head_dim = cosines.shape
    heads = projected.shape[1] // head_dim - 2
    slots = caches[0].shape[0]
    block = min(512, slots)
    part = jax.ShapeDtypeStruct((group, (heads + 1) * head_dim), bf16)
    new = jax.ShapeDtypeStruct((tokens, head_dim), bf16)
    return pl.pallas_call(
        functools.partial(
            attend_kernel,
            chips=chips,
            heads=heads,
            group=group,
            block=block,
            scale=1.0 / math.sqrt(head_dim),
        ),
        out_shape=[part] * chips + [new, new],
        in_specs=[in_smem, in_smem] + [in_vmem] * 8,
        out_specs=[in_vmem] * (chips + 2),
        scratch_shapes=[
            pltpu.VMEM((heads * tokens, head_dim), bf16),
            pltpu.VMEM((heads * tokens, head_dim), f32),
            pltpu.VMEM((heads * tokens, head_dim), f32),
            pltpu.VMEM((heads * tokens, head_dim), f32),
            pltpu.VMEM((tokens, (heads + 1) * head_dim), bf16),
        ],
        compiler_params=pltpu.CompilerParams(vmem_limit_bytes=40 << 20),
    )(place, fill, projected, cosines, sines, allowed, *caches)


def write_kernel(place, fill, owner, keys_new, values_new, keys, values, keys_out, values_out, *, window):
    tokens = owner.shape[1]
    slots = keys.shape[0]
    owned = jnp.broadcast_to((owner[...] == place[3]).astype(f32), (8, tokens))
    earlier = lax.broadcasted_iota(jnp.int32, (tokens, tokens), 0) < lax.broadcasted_iota(
        jnp.int32, (tokens, tokens), 1
    )
    rank = jnp.dot(
        owned.astype(bf16), earlier.astype(f32).astype(bf16), preferred_element_type=f32
    )
    start = jnp.minimum((fill[0] // 16) * 16, slots - window)
    start = pl.multiple_of(start, 16)
    target = rank[:1, :].astype(jnp.int32) + (fill[0] - start)
    row = lax.broadcasted_iota(jnp.int32, (window, tokens), 0)
    placement = jnp.where((row == target) & (owned[:1, :] > 0.0), 1.0, 0.0)
    written = jnp.sum(placement, 1, keepdims=True) > 0.0
    placement = placement.astype(bf16)
    for new, cache, out in ((keys_new, keys, keys_out), (values_new, values, values_out)):
        out[...] = cache[...]
        placed = jnp.dot(placement, new[...], preferred_element_type=f32)
        old = cache[pl.ds(start, window), :].astype(f32)
        out[pl.ds(start, window), :] = jnp.where(written, placed, old).astype(bf16)


def write(place, fill, owner, keys_new, values_new, keys, values, window):
    out = jax.ShapeDtypeStruct(keys.shape, keys.dtype)
    return pl.pallas_call(
        functools.partial(write_kernel, window=window),
        out_shape=(out, out),
        in_specs=[in_smem, in_smem] + [in_vmem] * 5,
        out_specs=(in_vmem, in_vmem),
        compiler_params=pltpu.CompilerParams(vmem_limit_bytes=16 << 20),
    )(place, fill, owner, keys_new, values_new, keys, values)


def merge_kernel(place, *refs, chips, heads, head_dim):
    parts, mine, other, merged = refs[:chips], *refs[chips:]
    rows = mine.shape[0]
    logs = []
    for part in parts:
        tail = part[:, heads * head_dim :].astype(f32)
        logs.append(
            tail[:, :heads] + tail[:, heads : 2 * heads] + tail[:, 2 * heads : 3 * heads]
        )
    top = functools.reduce(jnp.maximum, logs)
    shares = [jnp.exp2(level - top) for level in logs]
    whole = functools.reduce(jnp.add, shares)
    shares = [share / whole for share in shares]
    for head in range(heads):
        at = slice(head * head_dim, (head + 1) * head_dim)
        merged[:, at] = functools.reduce(
            jnp.add,
            [
                part[:, at].astype(f32) * share[:, head : head + 1]
                for part, share in zip(parts, shares)
            ],
        ).astype(bf16)
    core = place[0]
    mine[...] = merged[pl.ds(pl.multiple_of(core * rows, rows), rows), :]
    other[...] = merged[pl.ds(pl.multiple_of((1 - core) * rows, rows), rows), :]


def merge(place, parts, head_dim):
    group, width = parts[0].shape
    heads = width // head_dim - 1
    out = jax.ShapeDtypeStruct((group // 2, heads * head_dim), bf16)
    return pl.pallas_call(
        functools.partial(merge_kernel, chips=len(parts), heads=heads, head_dim=head_dim),
        out_shape=(out, out),
        in_specs=[in_smem] + [in_vmem] * len(parts),
        out_specs=(in_vmem, in_vmem),
        scratch_shapes=[pltpu.VMEM((group, heads * head_dim), bf16)],
    )(place, *parts)


def body(tokens, qkv_weight, cache_keys, cache_values, cache_fill, slot_owner, new_positions):
    peer_count = lax.axis_size("ctx")
    peer_index = lax.axis_index("ctx")
    lane_count = lax.axis_size("kv")
    lane_index = lax.axis_index("kv")
    chips = peer_count // 2
    core = peer_index % 2
    chip = peer_index // 2
    head_dim = cache_keys.shape[1]
    total_new = slot_owner.shape[0]
    new_local = total_new // peer_count
    group = 2 * new_local
    capacity = max(2, 2 * new_local // peer_count)
    window = -(-(capacity * peer_count) // 16) * 16 + 16

    def swap(value):
        return lax.ppermute(value, "ctx", [(i, i ^ 1) for i in range(peer_count)])

    def exchange(value, hop):
        return lax.ppermute(value, "ctx", [(i, i ^ (2 * hop)) for i in range(peer_count)])

    parts = [tokens] + [
        lax.ppermute(tokens, "kv", [(i, i ^ hop) for i in range(lane_count)])
        for hop in range(1, lane_count)
    ]
    sibling_keys = swap(cache_keys)
    sibling_values = swap(cache_values)

    place = jnp.stack([core, lane_index, chip, peer_index]).astype(jnp.int32)
    peer_iota = jnp.arange(peer_count, dtype=jnp.int32)
    own_fill = jnp.sum(jnp.where(peer_iota == peer_index, cache_fill, 0))
    sibling_fill = jnp.sum(jnp.where(peer_iota == (peer_index ^ 1), cache_fill, 0))
    fill = jnp.stack([own_fill, sibling_fill])
    absolute = jnp.sum(cache_fill) + new_positions
    half_dim = head_dim // 2
    freqs = jnp.exp(
        jnp.arange(half_dim, dtype=f32) * (-2.0 * math.log(rope_base) / head_dim)
    )
    angles = absolute.astype(f32)[:, None] * freqs[None, :]
    cosines = jnp.cos(angles)
    sines = jnp.sin(angles)
    cosines = jnp.concatenate([cosines, cosines], 1)
    sines = jnp.concatenate([-sines, sines], 1)
    block_of = jnp.arange(total_new, dtype=jnp.int32) // group
    allowed = (
        (new_positions[None, :] <= new_positions[:, None]) & (block_of[None, :] == chip)
    ).astype(f32)

    keep, send = project(place, parts, qkv_weight, 2 * head_dim)
    chip_sum = keep + swap(send)
    outgoing = chip_sum.astype(jnp.float16)
    projected = chip_sum
    for hop in range(1, chips):
        projected = projected + exchange(outgoing, hop).astype(f32)

    *partial, keys_new, values_new = attend(
        place,
        fill,
        projected,
        cosines,
        sines,
        allowed,
        (cache_keys, sibling_keys, cache_values, sibling_values),
        chips,
        group,
    )
    received = [partial[0]] + [exchange(partial[hop], hop) for hop in range(1, chips)]
    keys_after, values_after = write(
        place,
        fill,
        slot_owner.reshape(1, total_new),
        keys_new,
        values_new,
        cache_keys,
        cache_values,
        window,
    )
    mine, other = merge(place, received, head_dim)
    theirs = swap(other)
    attended = jnp.where(
        core == 0, jnp.concatenate([mine, theirs], 1), jnp.concatenate([theirs, mine], 1)
    )
    return (attended, keys_after, values_after)


def solution(mesh):
    placed = (P("kv", "ctx"), P("ctx", "kv"), P("ctx", "kv"), P("ctx", "kv"), P(), P(), P())
    return jax.shard_map(
        body,
        mesh=mesh,
        in_specs=placed,
        out_specs=(P("ctx", "kv"), P("ctx", "kv"), P("ctx", "kv")),
        check_vma=False,
    )
```

```python
import functools
import math

import jax
import jax.numpy as jnp
from jax import lax
from jax.experimental import pallas as pl
from jax.experimental.pallas import tpu as pltpu
from jax.sharding import PartitionSpec as P

rope_base = 500000.0
lowest = -1e30
f32, bf16 = jnp.float32, jnp.bfloat16
in_vmem = pl.BlockSpec(memory_space=pltpu.VMEM)
in_smem = pl.BlockSpec(memory_space=pltpu.SMEM)


def load_kernel(tokens, weight, held, product, arrived, *, pieces):
    depth = weight.shape[0] // pieces

    def piece(i):
        rows = pl.ds(i * depth, depth)
        return pltpu.make_async_copy(weight.at[rows], held.at[rows], arrived.at[i])

    for i in range(pieces):
        piece(i).start()
    for i in range(pieces):
        piece(i).wait()
        at = slice(i * depth, (i + 1) * depth)
        partial = jnp.dot(tokens[:, at], held[at, :], preferred_element_type=f32)
        if i == 0:
            product[...] = partial
        else:
            product[...] += partial


def load(tokens, weight):
    pieces = 4
    return pl.pallas_call(
        functools.partial(load_kernel, pieces=pieces),
        out_shape=(
            pltpu.VMEM(weight.shape, bf16),
            jax.ShapeDtypeStruct((tokens.shape[0], weight.shape[1]), f32),
        ),
        in_specs=[in_vmem, pl.BlockSpec(memory_space=pltpu.HBM)],
        out_specs=(in_vmem, in_vmem),
        scratch_shapes=[pltpu.SemaphoreType.DMA((pieces,))],
        compiler_params=pltpu.CompilerParams(vmem_limit_bytes=16 << 20),
    )(tokens, weight)


def project_kernel(place, *refs, ready, half, tail):
    done, refs = (refs[0], refs[1:]) if ready else (None, refs)
    parts, (weight, keep, send, sums) = refs[:-4], refs[-4:]
    rows = parts[0].shape[0]
    gathered = jnp.concatenate([part[...] for part in parts], 0)
    product = jnp.dot(gathered, weight[...], preferred_element_type=f32)
    if ready:
        product = jnp.concatenate([done[...], product], 0)
    count = len(parts) + ready
    for hop in range(count):
        start = pl.multiple_of(((place[1] % count) ^ hop) * rows, rows)
        sums[pl.ds(start, rows), :] = product[hop * rows : (hop + 1) * rows, :]
    send[:, half:] = sums[:, 2 * half :]
    keep[:, half:] = sums[:, 2 * half :]
    for core, (first, second) in enumerate(((keep, send), (send, keep))):

        @pl.when(place[0] == core)
        def _(first=first, second=second):
            first[:, :half] = sums[:, :half]
            second[:, :half] = sums[:, half : 2 * half]


def project(place, done, parts, weight, head_dim):
    rows, columns = parts[0].shape[0], weight.shape[1]
    ready = done is not None
    count = len(parts) + ready
    half, tail = (columns - 2 * head_dim) // 2, 2 * head_dim
    out = jax.ShapeDtypeStruct((count * rows, half + tail), f32)
    return pl.pallas_call(
        functools.partial(project_kernel, ready=ready, half=half, tail=tail),
        out_shape=(out, out),
        in_specs=[in_smem] + [in_vmem] * (count + 1),
        out_specs=(in_vmem, in_vmem),
        scratch_shapes=[pltpu.VMEM((count * rows, columns), f32)],
        compiler_params=pltpu.CompilerParams(vmem_limit_bytes=16 << 20),
    )(place, *([done] if ready else []), *parts, weight)


def pack(mixed, total, peak, packed, heads, tokens, factor):
    head_dim = mixed.shape[1]
    lane = lax.broadcasted_iota(jnp.int32, (tokens, head_dim), 1)
    logs = jnp.zeros((tokens, head_dim), f32)
    for head in range(heads):
        at = slice(head * tokens, (head + 1) * tokens)
        denominator = jnp.sum(total[at, :], 1, keepdims=True)
        packed[:, head * head_dim : (head + 1) * head_dim] = (mixed[at, :] / denominator).astype(
            bf16
        )
        level = peak[at, :] * factor + jnp.log2(denominator)
        logs = jnp.where(lane % heads == head, level, logs)
    first = logs.astype(bf16).astype(f32)
    second = (logs - first).astype(bf16).astype(f32)
    third = logs - first - second
    packed[:, heads * head_dim :] = jnp.where(
        lane < heads, first, jnp.where(lane < 2 * heads, second, third)
    ).astype(bf16)


def columns_of(array, width):
    return [array[:, i * width : (i + 1) * width] for i in range(array.shape[1] // width)]


def score(rows, keys):
    return lax.dot_general(rows, keys, (((1,), (1,)), ((), ())), preferred_element_type=f32)


def attend_kernel(place, fill, projected, cosines, sines, keys, values, *refs, heads, block, factor, order):
    packed, keys_new, values_new, query_out, query, peak, total, mixed = refs
    tokens, head_dim = projected.shape[0], keys.shape[1]
    slots = keys.shape[0] // 2
    start = pl.multiple_of((place[4] ^ order) * tokens, tokens)
    cosine, sine = cosines[pl.ds(start, tokens), :], sines[pl.ds(start, tokens), :]

    def rotated(column):
        u = projected[:, column * head_dim : (column + 1) * head_dim]
        return (u * cosine + pltpu.roll(u, head_dim // 2, 1) * sine).astype(bf16)

    for head in range(heads):
        turned = rotated(head)
        query[head * tokens : (head + 1) * tokens, :] = turned
        query_out[:, head * head_dim : (head + 1) * head_dim] = turned
    keys_new[...] = rotated(heads)
    values_new[...] = projected[:, (heads + 1) * head_dim :].astype(bf16)
    peak[...] = jnp.full_like(peak, lowest)
    total[...] = jnp.zeros_like(total)
    mixed[...] = jnp.zeros_like(mixed)
    own_blocks = (fill[0] + block - 1) // block
    all_blocks = own_blocks + (fill[1] + block - 1) // block

    @pl.loop(0, all_blocks)
    def _(step):
        second = step >= own_blocks
        first_slot = jnp.where(second, slots + (step - own_blocks) * block, step * block)
        first_slot = pl.multiple_of(first_slot, block)
        limit = jnp.where(second, slots + fill[1], fill[0])
        slot = first_slot + lax.broadcasted_iota(jnp.int32, (1, block), 1)
        scores = score(query[...], keys[pl.ds(first_slot, block), :])
        scores = jnp.where(slot < limit, scores, lowest)
        parts = columns_of(scores, head_dim)
        before = peak[...]
        top = functools.reduce(jnp.maximum, parts)
        top = jnp.maximum(before, jnp.max(top, 1, keepdims=True))
        rescale = jnp.exp2((before - top) * factor)
        weights = [jnp.exp2((part - top) * factor) for part in parts]
        peak[...] = top
        total[...] = total[...] * rescale + functools.reduce(jnp.add, weights)
        weights = jnp.concatenate([weight.astype(bf16) for weight in weights], 1)
        mixed[...] = mixed[...] * rescale + jnp.dot(
            weights, values[pl.ds(first_slot, block), :], preferred_element_type=f32
        )

    pack(mixed, total, peak, packed, heads, tokens, factor)


def attend(place, fill, projected, cosines, sines, keys, values, order):
    tokens, head_dim = projected.shape[0], keys.shape[1]
    heads = projected.shape[1] // head_dim - 2
    block = min(512, keys.shape[0] // 2)
    new = jax.ShapeDtypeStruct((tokens, head_dim), bf16)
    state = pltpu.VMEM((heads * tokens, head_dim), f32)
    return pl.pallas_call(
        functools.partial(
            attend_kernel,
            heads=heads,
            block=block,
            factor=math.log2(math.e) / math.sqrt(head_dim),
            order=order,
        ),
        out_shape=(
            jax.ShapeDtypeStruct((tokens, (heads + 1) * head_dim), bf16),
            new,
            new,
            jax.ShapeDtypeStruct((tokens, heads * head_dim), bf16),
        ),
        in_specs=[in_smem, in_smem] + [in_vmem] * 5,
        out_specs=[in_vmem] * 4,
        scratch_shapes=[pltpu.VMEM((heads * tokens, head_dim), bf16), state, state, state],
        compiler_params=pltpu.CompilerParams(vmem_limit_bytes=28 << 20),
    )(place, fill, projected, cosines, sines, keys, values)


def sort_kernel(place, near, far, *outs, group):
    half = near.shape[0]
    for hop, out in enumerate(outs):
        start = (place[2] ^ hop) * group
        inside = pl.multiple_of(start % half, group)

        @pl.when(start // half == place[4])
        def _(out=out, inside=inside):
            out[...] = near[pl.ds(inside, group), :]

        @pl.when(start // half != place[4])
        def _(out=out, inside=inside):
            out[...] = far[pl.ds(inside, group), :]


def sort(place, near, far, chips, group):
    part = jax.ShapeDtypeStruct((group, near.shape[1]), near.dtype)
    return pl.pallas_call(
        functools.partial(sort_kernel, group=group),
        out_shape=[part] * chips,
        in_specs=[in_smem] + [in_vmem] * 2,
        out_specs=[in_vmem] * chips,
        compiler_params=pltpu.CompilerParams(vmem_limit_bytes=8 << 20),
    )(place, near, far)


def write_kernel(
    place, fill, owner, allowed, near_keys, far_keys, near_values, far_values, near_query, far_query, keys, values,
    keys_out, values_out, packed, keys_new, values_new, own_query, query, peak, total, mixed, *, window, factor
):
    tokens, head_dim = owner.shape[1], keys.shape[1]
    slots, half, group = keys.shape[0], near_keys.shape[0], allowed.shape[0]
    heads = query.shape[0] // group
    near_at = pl.multiple_of(place[4] * half, half)
    far_at = pl.multiple_of((1 - place[4]) * half, half)
    keys_new[pl.ds(near_at, half), :] = near_keys[...]
    keys_new[pl.ds(far_at, half), :] = far_keys[...]
    values_new[pl.ds(near_at, half), :] = near_values[...]
    values_new[pl.ds(far_at, half), :] = far_values[...]

    start = place[2] * group
    inside = pl.multiple_of(start % half, group)

    @pl.when(start // half == place[4])
    def _():
        own_query[...] = near_query[pl.ds(inside, group), :]

    @pl.when(start // half != place[4])
    def _():
        own_query[...] = far_query[pl.ds(inside, group), :]

    for head in range(heads):
        query[head * group : (head + 1) * group, :] = own_query[
            :, head * head_dim : (head + 1) * head_dim
        ]
    seen = jnp.concatenate([allowed[...]] * heads, 0) > 0.0
    scores = jnp.where(seen, score(query[...], keys_new[...]), lowest)
    top = jnp.max(scores, 1, keepdims=True)
    weights = jnp.where(seen, jnp.exp2((scores - top) * factor), 0.0)
    peak[...] = jnp.broadcast_to(top, peak.shape)
    total[...] = functools.reduce(jnp.add, columns_of(weights, head_dim))
    mixed[...] = jnp.dot(weights.astype(bf16), values_new[...], preferred_element_type=f32)
    pack(mixed, total, peak, packed, heads, group, factor)

    owned = jnp.broadcast_to((owner[...] == place[3]).astype(f32), (8, tokens))
    earlier = lax.broadcasted_iota(jnp.int32, (tokens, tokens), 0) < lax.broadcasted_iota(
        jnp.int32, (tokens, tokens), 1
    )
    rank = jnp.dot(
        owned.astype(bf16), earlier.astype(f32).astype(bf16), preferred_element_type=f32
    )
    start = jnp.minimum((fill[0] // 16) * 16, slots - window)
    start = pl.multiple_of(start, 16)
    target = rank[:1, :].astype(jnp.int32) + (fill[0] - start)
    row = lax.broadcasted_iota(jnp.int32, (window, tokens), 0)
    placement = jnp.where((row == target) & (owned[:1, :] > 0.0), 1.0, 0.0)
    written = jnp.sum(placement, 1, keepdims=True) > 0.0
    placement = placement.astype(bf16)
    for new, cache, out in ((keys_new, keys, keys_out), (values_new, values, values_out)):
        out[...] = cache[...]
        placed = jnp.dot(placement, new[...], preferred_element_type=f32)
        old = cache[pl.ds(start, window), :].astype(f32)
        out[pl.ds(start, window), :] = jnp.where(written, placed, old).astype(bf16)


def write(place, fill, owner, allowed, news, caches, window):
    out = jax.ShapeDtypeStruct(caches[0].shape, caches[0].dtype)
    group, tokens = allowed.shape
    head_dim, width = caches[0].shape[1], news[-1].shape[1]
    rows = group * (width // head_dim)
    new, state = pltpu.VMEM((tokens, head_dim), bf16), pltpu.VMEM((rows, head_dim), f32)
    return pl.pallas_call(
        functools.partial(
            write_kernel, window=window, factor=math.log2(math.e) / math.sqrt(head_dim)
        ),
        out_shape=(out, out, jax.ShapeDtypeStruct((group, width + head_dim), bf16)),
        in_specs=[in_smem, in_smem] + [in_vmem] * 10,
        out_specs=(in_vmem, in_vmem, in_vmem),
        scratch_shapes=[
            new,
            new,
            pltpu.VMEM((group, width), bf16),
            pltpu.VMEM((rows, head_dim), bf16),
            state,
            state,
            state,
        ],
        compiler_params=pltpu.CompilerParams(vmem_limit_bytes=16 << 20),
    )(place, fill, owner, allowed, *news, *caches)


def merge_kernel(place, *refs, chips, heads, head_dim):
    parts, mine, other, merged = refs[:chips], *refs[chips:]
    rows = mine.shape[0]
    logs = []
    for part in parts:
        tail = part[:, heads * head_dim :].astype(f32)
        logs.append(
            tail[:, :heads] + tail[:, heads : 2 * heads] + tail[:, 2 * heads : 3 * heads]
        )
    top = functools.reduce(jnp.maximum, logs)
    shares = [jnp.exp2(level - top) for level in logs]
    whole = functools.reduce(jnp.add, shares)
    shares = [share / whole for share in shares]
    for head in range(heads):
        at = slice(head * head_dim, (head + 1) * head_dim)
        merged[:, at] = functools.reduce(
            jnp.add,
            [
                part[:, at].astype(f32) * share[:, head : head + 1]
                for part, share in zip(parts, shares)
            ],
        ).astype(bf16)
    core = place[0]
    mine[...] = merged[pl.ds(pl.multiple_of(core * rows, rows), rows), :]
    other[...] = merged[pl.ds(pl.multiple_of((1 - core) * rows, rows), rows), :]


def merge(place, parts, head_dim):
    group, width = parts[0].shape
    heads = width // head_dim - 1
    out = jax.ShapeDtypeStruct((group // 2, heads * head_dim), bf16)
    return pl.pallas_call(
        functools.partial(merge_kernel, chips=len(parts), heads=heads, head_dim=head_dim),
        out_shape=(out, out),
        in_specs=[in_smem] + [in_vmem] * len(parts),
        out_specs=(in_vmem, in_vmem),
        scratch_shapes=[pltpu.VMEM((group, heads * head_dim), bf16)],
        compiler_params=pltpu.CompilerParams(vmem_limit_bytes=8 << 20),
    )(place, *parts)


def join_kernel(place, mine, theirs, out):
    width = mine.shape[1]
    for core, (first, second) in enumerate(((mine, theirs), (theirs, mine))):

        @pl.when(place[0] == core)
        def _(first=first, second=second):
            out[:, :width] = first[...]
            out[:, width:] = second[...]


def join(place, mine, theirs):
    return pl.pallas_call(
        join_kernel,
        out_shape=jax.ShapeDtypeStruct((mine.shape[0], 2 * mine.shape[1]), mine.dtype),
        in_specs=[in_smem] + [in_vmem] * 2,
        out_specs=in_vmem,
        compiler_params=pltpu.CompilerParams(vmem_limit_bytes=4 << 20),
    )(place, mine, theirs)


def body(tokens, qkv_weight, cache_keys, cache_values, cache_fill, slot_owner, new_positions):
    peer_count = lax.axis_size("ctx")
    peer_index = lax.axis_index("ctx")
    lane_count = lax.axis_size("kv")
    lane_index = lax.axis_index("kv")
    chips = peer_count // 2
    core = peer_index % 2
    chip = peer_index // 2
    head_dim = cache_keys.shape[1]
    total_new = slot_owner.shape[0]
    new_local = total_new // peer_count
    group = 2 * new_local
    capacity = max(2, 2 * new_local // peer_count)
    window = -(-(capacity * peer_count) // 16) * 16 + 16

    def swap(value):
        return lax.ppermute(value, "ctx", [(i, i ^ 1) for i in range(peer_count)])

    def exchange(value, hop):
        return lax.ppermute(value, "ctx", [(i, i ^ (2 * hop)) for i in range(peer_count)])

    parts = [tokens] + [
        lax.ppermute(tokens, "kv", [(i, i ^ hop) for i in range(lane_count)])
        for hop in range(1, lane_count)
    ]
    sibling_keys = swap(cache_keys)
    sibling_values = swap(cache_values)

    half_lanes = lane_count // 2
    upper = lane_index // half_lanes
    place = jnp.stack([core, lane_index, chip, peer_index, upper]).astype(jnp.int32)
    peer_iota = jnp.arange(peer_count, dtype=jnp.int32)
    own_fill = jnp.sum(jnp.where(peer_iota == peer_index, cache_fill, 0))
    sibling_fill = jnp.sum(jnp.where(peer_iota == (peer_index ^ 1), cache_fill, 0))
    fill = jnp.stack([own_fill, sibling_fill])
    absolute = jnp.sum(cache_fill) + new_positions
    half_dim = head_dim // 2
    freqs = jnp.exp(
        jnp.arange(half_dim, dtype=f32) * (-2.0 * math.log(rope_base) / head_dim)
    )
    angles = absolute.astype(f32)[:, None] * freqs[None, :]
    cosines = jnp.cos(angles)
    sines = jnp.sin(angles)
    cosines = jnp.concatenate([cosines, cosines], 1)
    sines = jnp.concatenate([-sines, sines], 1)
    own_rows = lax.dynamic_slice_in_dim(new_positions, chip * group, group)
    allowed = (new_positions[None, :] <= own_rows[:, None]).astype(f32)
    keys_both = jnp.concatenate([cache_keys, sibling_keys], 0)
    values_both = jnp.concatenate([cache_values, sibling_values], 0)

    held, own_product = load(tokens, qkv_weight)

    def summed(done, chunk):
        keep, send = project(place, done, chunk, held, head_dim)
        chip_sum = keep + swap(send)
        outgoing = chip_sum.astype(jnp.float16)
        whole = chip_sum
        for hop in range(1, chips):
            whole = whole + exchange(outgoing, hop).astype(f32)
        return whole

    near = summed(own_product, parts[1:half_lanes])
    far = summed(None, parts[half_lanes:])
    near_packed, near_keys, near_values, near_query = attend(
        place, fill, near, cosines, sines, keys_both, values_both, 0
    )
    far_packed, far_keys, far_values, far_query = attend(
        place, fill, far, cosines, sines, keys_both, values_both, 1
    )
    partial = sort(place, near_packed, far_packed, chips, group)
    received = [partial[0]] + [exchange(partial[hop], hop) for hop in range(1, chips)]
    keys_after, values_after, new_part = write(
        place,
        fill,
        slot_owner.reshape(1, total_new),
        allowed,
        (near_keys, far_keys, near_values, far_values, near_query, far_query),
        (cache_keys, cache_values),
        window,
    )
    mine, other = merge(place, received + [new_part], head_dim)
    attended = join(place, mine, swap(other))
    return (attended, keys_after, values_after)


def solution(mesh):
    placed = (P("kv", "ctx"), P("ctx", "kv"), P("ctx", "kv"), P("ctx", "kv"), P(), P(), P())
    return jax.shard_map(
        body,
        mesh=mesh,
        in_specs=placed,
        out_specs=(P("ctx", "kv"), P("ctx", "kv"), P("ctx", "kv")),
        check_vma=False,
    )
```

```python
import functools
import math

import jax
import jax.numpy as jnp
from jax import lax
from jax.experimental import pallas as pl
from jax.experimental.pallas import tpu as pltpu
from jax.sharding import PartitionSpec as P

rope_base = 500000.0
lowest = -1e30
f32, bf16 = jnp.float32, jnp.bfloat16
in_vmem = pl.BlockSpec(memory_space=pltpu.VMEM)
in_smem = pl.BlockSpec(memory_space=pltpu.SMEM)


def hold_kernel(weight, held, arrived, *, pieces):
    depth = weight.shape[0] // pieces

    def piece(i):
        at = pl.ds(i * depth, depth)
        return pltpu.make_async_copy(weight.at[at], held.at[at], arrived.at[i])

    for i in range(pieces):
        piece(i).start()
    for i in range(pieces):
        piece(i).wait()


def hold(weight):
    pieces = 4
    return pl.pallas_call(
        functools.partial(hold_kernel, pieces=pieces),
        out_shape=pltpu.VMEM(weight.shape, bf16),
        in_specs=[pl.BlockSpec(memory_space=pltpu.HBM)],
        out_specs=in_vmem,
        scratch_shapes=[pltpu.SemaphoreType.DMA((pieces,))],
        compiler_params=pltpu.CompilerParams(vmem_limit_bytes=2 << 20),
    )(weight)


def project_kernel(*refs, half):
    core, lane = lax.axis_index("ctx") & 1, lax.axis_index("kv")
    parts, (weight, early_keep, early_send, keep, send, sums) = refs[:-6], refs[-6:]
    early = early_keep.shape[1]
    rows = parts[0].shape[0]
    gathered = jnp.concatenate([part[...] for part in parts], 0)
    sums[...] = jnp.dot(gathered, weight[...], preferred_element_type=f32)
    for hop in range(len(parts)):
        start = pl.multiple_of((lane ^ hop) * rows, rows)
        to, at = pl.ds(start, rows), slice(hop * rows, (hop + 1) * rows)
        send[to, half - early :] = sums[at, 2 * half :]
        keep[to, half - early :] = sums[at, 2 * half :]
        kept, sent = (early_keep, keep), (early_send, send)
        for side, (first, second) in enumerate(((kept, sent), (sent, kept))):

            @pl.when(core == side)
            def _(first=first, second=second, to=to, at=at):
                first[0][to, :] = sums[at, :early]
                first[1][to, : half - early] = sums[at, early:half]
                second[0][to, :] = sums[at, half : half + early]
                second[1][to, : half - early] = sums[at, half + early : 2 * half]


def project(parts, weight, head_dim):
    rows, columns = parts[0].shape[0], weight.shape[1]
    half, tail = (columns - 2 * head_dim) // 2, 2 * head_dim
    early = half // head_dim // 2 * head_dim
    early_out = jax.ShapeDtypeStruct((len(parts) * rows, early), f32)
    out = jax.ShapeDtypeStruct((len(parts) * rows, half - early + tail), f32)
    return pl.pallas_call(
        functools.partial(project_kernel, half=half),
        out_shape=(early_out, early_out, out, out),
        in_specs=[in_vmem] * (len(parts) + 1),
        out_specs=(in_vmem,) * 4,
        scratch_shapes=[pltpu.VMEM((len(parts) * rows, columns), f32)],
        compiler_params=pltpu.CompilerParams(vmem_limit_bytes=12 << 20),
    )(*parts, weight)


def position_kernel(fill, offsets, positions):
    filled = fill[0]
    for i in range(1, fill.shape[0]):
        filled += fill[i]
    positions[...] = (offsets[...] + filled).astype(f32)


def position(fill, offsets):
    return pl.pallas_call(
        position_kernel,
        out_shape=jax.ShapeDtypeStruct(offsets.shape, f32),
        in_specs=[in_smem, in_vmem],
        out_specs=in_vmem,
        compiler_params=pltpu.CompilerParams(vmem_limit_bytes=4 << 20),
    )(fill, offsets)


def pack(mixed, total, peak, packed, heads, tokens, factor, offset):
    head_dim = mixed.shape[1]
    lane = lax.broadcasted_iota(jnp.int32, (tokens, head_dim), 1)
    logs = jnp.zeros((tokens, head_dim), f32)
    for head in range(heads):
        at = slice(head * tokens, (head + 1) * tokens)
        denominator = jnp.sum(total[at, :], 1, keepdims=True)
        packed[:, head * head_dim : (head + 1) * head_dim] = (mixed[at, :] / denominator).astype(
            bf16
        )
        level = peak[at, :] * factor + jnp.log2(denominator)
        logs = jnp.where(lane % heads == head, level, logs)
    first = logs.astype(bf16).astype(f32)
    second = (logs - first).astype(bf16).astype(f32)
    third = logs - first - second
    return jnp.where(
        lane < offset + heads, first, jnp.where(lane < offset + 2 * heads, second, third)
    )


def columns_of(array, width):
    return [array[:, i * width : (i + 1) * width] for i in range(array.shape[1] // width)]


def score(rows, keys):
    return lax.dot_general(rows, keys, (((1,), (1,)), ((), ())), preferred_element_type=f32)


def attend_kernel(fill, projected, cosines, sines, *refs, heads, block, factor, group, last):
    caches, refs = (refs[0:2], refs[2:4]), refs[4:]
    if last:
        early, refs = refs[0], refs[1:]
        (outs, (keys_new, values_new)), refs = (refs[:-8], refs[-8:-6]), refs[-6:]
        own_query, query, peak, total, mixed, packed = refs
    else:
        packed, own_query, query, peak, total, mixed = refs
    me = lax.axis_index("ctx")
    chip = me >> 1
    tokens, head_dim = cosines.shape
    cosine, sine = cosines[...], sines[...]

    def column_of(column):
        return projected[:, column * head_dim : (column + 1) * head_dim]

    def rotated(column):
        u = column_of(column)
        return (u * cosine + pltpu.roll(u, head_dim // 2, 1) * sine).astype(bf16)

    own = pl.multiple_of(chip * group, group)
    for head in range(heads):
        query[head * tokens : (head + 1) * tokens, :] = rotated(head)
        own_query[head * group : (head + 1) * group, :] = query[
            pl.ds(head * tokens + own, group), :
        ]
    if last:
        keys_new[...] = rotated(heads)
        values_new[...] = column_of(heads + 1).astype(bf16)
    peak[...] = jnp.full_like(peak, lowest)
    total[...] = jnp.zeros_like(total)
    mixed[...] = jnp.zeros_like(mixed)

    for which, (keys, values) in enumerate(caches):
        filled = fill[me ^ which]

        def advance(first_slot, size, keys=keys, values=values, filled=filled):
            slot = first_slot + lax.broadcasted_iota(jnp.int32, (1, size), 1)
            scores = score(query[...], keys[pl.ds(first_slot, size), :])
            scores = jnp.where(slot < filled, scores, lowest)
            parts = columns_of(scores, head_dim)
            before = peak[...]
            top = functools.reduce(jnp.maximum, parts)
            top = jnp.maximum(before, jnp.max(top, 1, keepdims=True))
            rescale = jnp.exp2((before - top) * factor)
            weights = [jnp.exp2((part - top) * factor) for part in parts]
            peak[...] = top
            total[...] = total[...] * rescale + functools.reduce(jnp.add, weights)
            weights = jnp.concatenate([weight.astype(bf16) for weight in weights], 1)
            mixed[...] = mixed[...] * rescale + jnp.dot(
                weights, values[pl.ds(first_slot, size), :], preferred_element_type=f32
            )

        whole = (filled + block // 2 - 1) // block

        @pl.loop(0, whole)
        def _(step, advance=advance):
            advance(pl.multiple_of(step * block, block), block)

        @pl.when(whole * block < filled)
        def _(advance=advance, whole=whole):
            advance(pl.multiple_of(whole * block, block), block // 2)

    offset = 3 * heads * last
    tail = pack(mixed, total, peak, packed, heads, tokens, factor, offset)
    split = heads * head_dim
    if last:
        lane = lax.broadcasted_iota(jnp.int32, tail.shape, 1)
        tail = jnp.where(lane < offset, early[:, split:].astype(f32), tail)
    packed[:, split:] = tail.astype(bf16)
    if last:
        for hop, out in enumerate(outs):
            at = pl.ds(pl.multiple_of((chip ^ hop) * group, group), group)
            out[:, :split] = early[at, :split]
            out[:, split:] = packed[at, :]


def attend(fill, projected, cosines, sines, caches, early, chips, group):
    tokens, (slots, head_dim) = projected.shape[0], caches[0].shape
    last = early is not None
    heads = projected.shape[1] // head_dim - 2 * last
    width = (heads + 1) * head_dim
    half = jax.ShapeDtypeStruct((tokens, width), bf16)
    new = jax.ShapeDtypeStruct((tokens, head_dim), bf16)
    own = jax.ShapeDtypeStruct((heads * group, head_dim), bf16)
    part = jax.ShapeDtypeStruct((group, width + heads * head_dim), bf16)
    outs = [part] * chips + [new, new, own] if last else [half, own]
    state = pltpu.VMEM((heads * tokens, head_dim), f32)
    return pl.pallas_call(
        functools.partial(
            attend_kernel,
            heads=heads,
            block=min(1024 if tokens <= 128 else 512, slots),
            factor=math.log2(math.e) / math.sqrt(head_dim),
            group=group,
            last=last,
        ),
        out_shape=outs,
        in_specs=[in_smem] + [in_vmem] * (7 + last),
        out_specs=[in_vmem] * len(outs),
        scratch_shapes=[pltpu.VMEM((heads * tokens, head_dim), bf16), state, state, state]
        + [pltpu.VMEM(half.shape, bf16)] * last,
        compiler_params=pltpu.CompilerParams(vmem_limit_bytes=(8 + tokens // 16) << 20),
    )(fill, projected, cosines, sines, *caches, *([early] if last else []))


def write_kernel(
    fill, owner, offsets, keys_new, values_new, early_query, late_query, keys, values,
    keys_out, values_out, packed, peak, total, mixed, *, window, factor
):
    tokens, head_dim = owner.shape[1], keys.shape[1]
    slots, group = keys.shape[0], packed.shape[0]
    query = jnp.concatenate([early_query[...], late_query[...]], 0)
    heads = query.shape[0] // group
    me = lax.axis_index("ctx")
    own = (me >> 1) * group + lax.broadcasted_iota(jnp.int32, (group, tokens), 0)
    same = own == lax.broadcasted_iota(jnp.int32, (group, tokens), 1)
    offset = offsets[...].astype(f32)
    own_offset = jnp.sum(jnp.where(same, offset, 0.0), 1, keepdims=True)
    allowed = jnp.where(offset <= own_offset, 1.0, 0.0)
    seen = jnp.concatenate([allowed] * heads, 0) > 0.0
    scores = jnp.where(seen, score(query, keys_new[...]), lowest)
    top = jnp.max(scores, 1, keepdims=True)
    weights = jnp.where(seen, jnp.exp2((scores - top) * factor), 0.0)
    peak[...] = jnp.broadcast_to(top, peak.shape)
    total[...] = functools.reduce(jnp.add, columns_of(weights, head_dim))
    mixed[...] = jnp.dot(weights.astype(bf16), values_new[...], preferred_element_type=f32)
    half = heads // 2
    tails = []
    for index in range(2):
        at = pl.ds(index * half * group, half * group)
        to = packed.at[:, pl.ds(index * half * head_dim, half * head_dim)]
        state = (mixed.at[at], total.at[at], peak.at[at])
        tails.append(pack(*state, to, half, group, factor, 3 * half * index))
    lane = lax.broadcasted_iota(jnp.int32, tails[0].shape, 1)
    packed[:, heads * head_dim :] = jnp.where(lane < 3 * half, *tails).astype(bf16)

    owned = jnp.broadcast_to((owner[...] == me).astype(f32), (8, tokens))
    earlier = lax.broadcasted_iota(jnp.int32, (tokens, tokens), 0) < lax.broadcasted_iota(
        jnp.int32, (tokens, tokens), 1
    )
    rank = jnp.dot(
        owned.astype(bf16), earlier.astype(f32).astype(bf16), preferred_element_type=f32
    )
    filled = fill[me]
    start = pl.multiple_of(jnp.minimum((filled // 16) * 16, slots - window), 16)
    target = rank[:1, :].astype(jnp.int32) + (filled - start)
    row = lax.broadcasted_iota(jnp.int32, (window, tokens), 0)
    placement = jnp.where((row == target) & (owned[:1, :] > 0.0), 1.0, 0.0)
    written = jnp.sum(placement, 1, keepdims=True) > 0.0
    placement = placement.astype(bf16)
    for new, cache, out in ((keys_new, keys, keys_out), (values_new, values, values_out)):
        out[...] = cache[...]
        placed = jnp.dot(placement, new[...], preferred_element_type=f32)
        old = cache[pl.ds(start, window), :].astype(f32)
        out[pl.ds(start, window), :] = jnp.where(written, placed, old).astype(bf16)


def write(fill, owner, offsets, news, caches, group, window):
    out = jax.ShapeDtypeStruct(caches[0].shape, caches[0].dtype)
    head_dim = caches[0].shape[1]
    rows = news[-1].shape[0] + news[-2].shape[0]
    width = (rows // group + 1) * head_dim
    state = pltpu.VMEM((rows, head_dim), f32)
    return pl.pallas_call(
        functools.partial(
            write_kernel, window=window, factor=math.log2(math.e) / math.sqrt(head_dim)
        ),
        out_shape=(out, out, jax.ShapeDtypeStruct((group, width), bf16)),
        in_specs=[in_smem] + [in_vmem] * 8,
        out_specs=(in_vmem, in_vmem, in_vmem),
        scratch_shapes=[state, state, state],
        compiler_params=pltpu.CompilerParams(vmem_limit_bytes=12 << 20),
    )(fill, owner, offsets, *news, *caches)


def merge_kernel(*refs, chips, heads, head_dim):
    parts, mine, other, merged = refs[:chips], *refs[chips:]
    rows = mine.shape[0]
    count = heads // 2
    for half in range(2):
        start, end = half * count * head_dim, (half + 1) * count * head_dim
        blocks = [part[:, start:end].astype(f32) for part in parts]
        tails = [part[:, heads * head_dim :].astype(f32) for part in parts]
        tails = [tail[:, 3 * count * half : 3 * count * (half + 1)] for tail in tails]
        logs = [
            tail[:, :count] + tail[:, count : 2 * count] + tail[:, 2 * count :] for tail in tails
        ]
        top = functools.reduce(jnp.maximum, logs)
        shares = [jnp.exp2(level - top) for level in logs]
        whole = functools.reduce(jnp.add, shares)
        shares = [share / whole for share in shares]
        for head in range(count):
            at = slice(head * head_dim, (head + 1) * head_dim)
            start = (half * count + head) * head_dim
            merged[:, start : start + head_dim] = functools.reduce(
                jnp.add,
                [
                    block[:, at] * share[:, head : head + 1]
                    for block, share in zip(blocks, shares)
                ],
            ).astype(bf16)
    core = lax.axis_index("ctx") & 1
    mine[...] = merged[pl.ds(pl.multiple_of(core * rows, rows), rows), :]
    other[...] = merged[pl.ds(pl.multiple_of((1 - core) * rows, rows), rows), :]


def merge(parts, head_dim):
    group, width = parts[0].shape
    heads = width // head_dim - 1
    out = jax.ShapeDtypeStruct((group // 2, heads * head_dim), bf16)
    return pl.pallas_call(
        functools.partial(merge_kernel, chips=len(parts), heads=heads, head_dim=head_dim),
        out_shape=(out, out),
        in_specs=[in_vmem] * len(parts),
        out_specs=(in_vmem, in_vmem),
        scratch_shapes=[pltpu.VMEM((group, heads * head_dim), bf16)],
        compiler_params=pltpu.CompilerParams(vmem_limit_bytes=8 << 20),
    )(*parts)


def join_kernel(mine, theirs, out):
    width = mine.shape[1]
    core = lax.axis_index("ctx") & 1
    for side, (first, second) in enumerate(((mine, theirs), (theirs, mine))):

        @pl.when(core == side)
        def _(first=first, second=second):
            out[:, :width] = first[...]
            out[:, width:] = second[...]


def join(mine, theirs):
    return pl.pallas_call(
        join_kernel,
        out_shape=jax.ShapeDtypeStruct((mine.shape[0], 2 * mine.shape[1]), mine.dtype),
        in_specs=[in_vmem] * 2,
        out_specs=in_vmem,
        compiler_params=pltpu.CompilerParams(vmem_limit_bytes=4 << 20),
    )(mine, theirs)


def body(tokens, qkv_weight, cache_keys, cache_values, cache_fill, slot_owner, new_positions):
    peer_count = lax.axis_size("ctx")
    lane_count = lax.axis_size("kv")
    chips = peer_count // 2
    head_dim = cache_keys.shape[1]
    total_new = slot_owner.shape[0]
    new_local = total_new // peer_count
    group = 2 * new_local
    capacity = max(2, 2 * new_local // peer_count)
    window = -(-(capacity * peer_count) // 16) * 16 + 16

    def swap(value):
        return lax.ppermute(value, "ctx", [(i, i ^ 1) for i in range(peer_count)])

    def exchange(value, hop):
        return lax.ppermute(value, "ctx", [(i, i ^ (2 * hop)) for i in range(peer_count)])

    def across(value, hops):
        return [
            lax.ppermute(value, "kv", [(i, i ^ hop) for i in range(lane_count)]) for hop in hops
        ]

    parts = [tokens] + across(tokens, range(1, lane_count))
    sibling_keys = swap(cache_keys)
    sibling_values = swap(cache_values)
    caches = (cache_keys, cache_values, sibling_keys, sibling_values)

    offsets = new_positions.reshape(1, total_new)
    absolute = position(cache_fill, offsets).reshape(total_new)
    half_dim = head_dim // 2
    freqs = jnp.exp(
        jnp.arange(half_dim, dtype=f32) * (-2.0 * math.log(rope_base) / head_dim)
    )
    angles = absolute[:, None] * freqs[None, :]
    cosines = jnp.cos(angles)
    sines = jnp.sin(angles)
    cosines = jnp.concatenate([cosines, cosines], 1)
    sines = jnp.concatenate([-sines, sines], 1)

    early_keep, early_send, keep, send = project(parts, hold(qkv_weight), head_dim)
    early_sum, late_sum = early_keep + swap(early_send), keep + swap(send)
    hops = [1 << i for i in range(chips.bit_length() - 1)]
    def summed(value):
        for hop_pair in zip(hops, reversed(hops)):
            halved = (value * 0.5).astype(jnp.float16)
            pairs = [(i, i ^ (2 * hop_pair[i % 2])) for i in range(peer_count)]
            value = value + lax.ppermute(halved, "ctx", pairs).astype(f32) * 2.0
        return value

    early, early_query = attend(
        cache_fill, summed(early_sum), cosines, sines, caches, None, chips, group
    )
    *partial, keys_new, values_new, late_query = attend(
        cache_fill, summed(late_sum), cosines, sines, caches, early, chips, group
    )
    received = [partial[0]] + [exchange(partial[hop], hop) for hop in range(1, chips)]
    keys_after, values_after, new_part = write(
        cache_fill,
        slot_owner.reshape(1, total_new),
        offsets,
        (keys_new, values_new, early_query, late_query),
        (cache_keys, cache_values),
        group,
        window,
    )
    mine, other = merge(received + [new_part], head_dim)
    attended = join(mine, swap(other))
    return (attended, keys_after, values_after)


def solution(mesh):
    placed = (P("kv", "ctx"), P("ctx", "kv"), P("ctx", "kv"), P("ctx", "kv"), P(), P(), P())
    return jax.shard_map(
        body,
        mesh=mesh,
        in_specs=placed,
        out_specs=(P("ctx", "kv"), P("ctx", "kv"), P("ctx", "kv")),
        check_vma=False,
    )
```
